32 devices in a mesh: runs: 2 (over y), curve: 4 (over z), sub: 4 (over x, core).
Axes of the slice: x: 2, y: 2, z: 4, core: 2. Of those that a mesh axis runs over, the one named last changes fastest.
Arguments:
- positions: float32 [3, 16384, 128], P(None, ('runs', 'curve', 'sub')), parts along dimension 1, may hold values from -1 to 1
- strengths: float32 [3, 16384, 128], P(None, ('runs', 'curve', 'sub')), parts along dimension 1, may hold values from -6 to 6
- counts: int32 [16384], P(('runs', 'curve', 'sub')), parts along dimension 0, may hold values from 1 to 128
- frequencies: float32 [3, 128], replicated, may hold values from -3 to 3
- phases: float32 [128], replicated, may hold values from -3.140625 to 3.140625
- charge_dirs: float32 [3, 128], replicated, may hold values from -0.3125 to 0.3125
- velocity_dirs: float32 [3, 128], replicated, may hold values from -0.5 to 0.5
- up_maps: float32 [8, 128, 128], replicated, may hold values from -0.1875 to 0.1875
- down_maps: float32 [8, 128, 128], replicated, may hold values from -0.5 to 0.5
- far_maps: float32 [16, 128, 128], replicated, may hold values from -0.09375 to 0.09375
- coarse_maps: float32 [16, 128, 128], replicated, may hold values from -0.046875 to 0.046875
- send_boxes: int32 [512, 8], P(('runs', 'curve', 'sub')), parts along dimension 0, may hold values from 0 to 511
- far_source: int32 [16384, 32], P(('runs', 'curve', 'sub')), parts along dimension 0, may hold values from 0 to 1151, as said below
- far_class: int32 [16384, 32], P(('runs', 'curve', 'sub')), parts along dimension 0, may hold values from 0 to 15
- near_source: int32 [16384, 2], P(('runs', 'curve', 'sub')), parts along dimension 0, may hold values from 0 to 519, as said below
- coarse_class: int32 [256, 128], P(('runs', 'curve', 'sub')), parts along dimension 0, may hold values from 0 to 15
Outputs:
- velocity: float32 [3, 16384, 128], P(None, ('runs', 'curve', 'sub')), parts along dimension 1
The draws below stay inside these ranges and needn't reach their ends.
There are 2 independent parts, one for each index of `runs`. The reference program is written for one: setup_inputs(seed, part) draws one part's arguments, and reference() takes and returns one part's arrays. A program takes and returns all parts, laid end to end along the dimension named above; an argument that names none is the same for every part. Nothing has to cross between parts.
Inputs may be any that keep to these rules, and one draw needn't show every extreme that they name: `send_boxes`: local leaf box numbers of the sending device; any box may be sent several times or not at all. `far_source`: every received row 1024 to 1151 of a device's source table is named by exactly one entry of that device's boxes; all other entries name rows below 1024, the device's own boxes and the 256 boxes on each side along the curve. `near_source`: entry l of box r of a device is 4 + r + o with o a nonzero offset of at most 4 in size; entries may repeat.
All inputs are finite; a program needn't handle non-finite values.
Results may differ from the reference program's by a relative error of at most 0.0003.
Values sent between devices are 32-bit elements; how exact they have to be, the bound alone decides.
A program may use at most 64 MiB of HBM per device.

```python
import math
import jax
import jax.numpy as jnp
from jax import lax

K = 128
P_SIZE = 128
NCLASS = 16
NL = 32
NN = 2
HW = 4
CAP = 8
B_DEV = 512
MH = 256
NODES = 16
BOXES = 8192
TOPS = 128


def draw_far_source(key, part):
    key = jax.random.fold_in(key, 11)

    def one_device(device_key):
        first_key, second_key = jax.random.split(device_key)
        values = jax.random.randint(first_key, (B_DEV * NL,), 0, B_DEV + 2 * MH)
        order = jax.random.permutation(second_key, B_DEV * NL)
        forced = B_DEV + 2 * MH + jnp.arange(NODES * CAP, dtype=jnp.int32)
        values = values.at[order[:NODES * CAP]].set(forced)
        return values.reshape(B_DEV, NL)
    device_keys = jax.random.split(key, NODES)
    return jax.vmap(one_device)(device_keys).reshape(BOXES, NL).astype(jnp.int32)


def draw_near_source(key, part):
    key = jax.random.fold_in(key, 23)
    raw_offset = jax.random.randint(key, (NODES, B_DEV, NN), 0, 2 * HW)
    offset = jnp.where(raw_offset < HW, raw_offset - HW, raw_offset - HW + 1)
    base = HW + jnp.arange(B_DEV, dtype=jnp.int32)[None, :, None]
    extended = base + offset
    extended = extended.at[:, 0, 0].set(0)
    extended = extended.at[:, B_DEV - 1, 0].set(B_DEV + 2 * HW - 1)
    return extended.reshape(BOXES, NN).astype(jnp.int32)


def set_ends(drawn, own_key, smallest, largest):
    shape = drawn.shape
    spot = [jax.random.randint(jax.random.fold_in(own_key, axis), (), 0, shape[axis]) for axis in range(len(shape))]
    drawn = drawn.at[tuple(spot)].set(smallest)
    longest = shape.index(max(shape))
    spot[longest] = (spot[longest] + 1) % shape[longest]
    return drawn.at[tuple(spot)].set(largest)


def block_scale(stream_key, shape, shards, least, high):
    loudness, own = 1.0, jax.random.fold_in(stream_key, 6)
    for position, parts in shards:
        steps = jnp.exp(jax.random.uniform(jax.random.fold_in(own, position), (parts,), jnp.float32, least / len(shards), high / len(shards)))
        loudness = loudness * jnp.repeat(steps, shape[position] // parts).reshape([-1 if axis == position else 1 for axis in range(len(shape))])
    return loudness


def noise(stream_key, dims, scale, most, shards=(), kind=jnp.bfloat16):
    result = jax.random.normal(stream_key, dims, jnp.float32) * scale
    if len(shards) > 0:
        result = block_scale(stream_key, dims, shards, -0.22, 0.18) * result
    return jnp.clip(result, min=-most, max=most).astype(kind)


def setup_inputs(seed: int = 0, part: int = 0) -> dict:
    keys = jax.random.split(jax.random.key(seed), 17)
    own_keys = jax.random.split(jax.random.fold_in(keys[16], part), 17)
    positions = jnp.clip(jax.random.uniform(own_keys[0], (3, BOXES, P_SIZE), jnp.float32, -1.0, 1.0) * block_scale(own_keys[0], (3, BOXES, P_SIZE), ((1, 16),), -0.4, 0.0), -1.0, 1.0)
    strengths = noise(own_keys[1], (3, BOXES, P_SIZE), 1.0, 6.0, ((1, 16),), jnp.float32)
    counts = set_ends(jax.random.randint(own_keys[2], (BOXES,), 1, P_SIZE + 1), jax.random.fold_in(own_keys[2], 1), 1, P_SIZE).astype(jnp.int32)
    frequencies = jnp.clip(jax.random.uniform(keys[3], (3, K), jnp.float32, -3.0, 3.0), -3.0, 3.0)
    phases = jnp.clip(jax.random.uniform(keys[4], (K,), jnp.float32, -3.140625, 3.140625), -3.140625, 3.140625)
    charge_dirs = noise(keys[5], (3, K), (3 * P_SIZE) ** -0.5, 0.3125, (), jnp.float32)
    velocity_dirs = noise(keys[6], (3, K), K ** -0.5, 0.5, (), jnp.float32)
    up_maps = noise(keys[7], (8, K, K), (8 * K) ** -0.5, 0.1875, (), jnp.float32)
    down_maps = noise(keys[8], (8, K, K), K ** -0.5, 0.5, (), jnp.float32)
    far_maps = noise(keys[9], (NCLASS, K, K), (K * NL) ** -0.5, 0.09375, (), jnp.float32)
    coarse_maps = noise(keys[10], (NCLASS, K, K), (K * TOPS) ** -0.5, 0.046875, (), jnp.float32)
    send_boxes = set_ends(jax.random.randint(own_keys[11], (NODES * NODES, CAP), 0, B_DEV), jax.random.fold_in(own_keys[11], 1), 0, B_DEV - 1).astype(jnp.int32)
    far_source = draw_far_source(jax.random.fold_in(jax.random.fold_in(keys[16], part), 71), part)
    far_class = set_ends(jax.random.randint(own_keys[13], (BOXES, NL), 0, NCLASS), jax.random.fold_in(own_keys[13], 1), 0, NCLASS - 1).astype(jnp.int32)
    near_source = draw_near_source(jax.random.fold_in(jax.random.fold_in(keys[16], part), 71), part)
    coarse_class = set_ends(jax.random.randint(own_keys[15], (TOPS, TOPS), 0, NCLASS), jax.random.fold_in(own_keys[15], 1), 0, NCLASS - 1).astype(jnp.int32)
    return dict(positions=positions, strengths=strengths, counts=counts, frequencies=frequencies, phases=phases, charge_dirs=charge_dirs, velocity_dirs=velocity_dirs, up_maps=up_maps, down_maps=down_maps, far_maps=far_maps, coarse_maps=coarse_maps, send_boxes=send_boxes, far_source=far_source, far_class=far_class, near_source=near_source, coarse_class=coarse_class)


highest = lax.Precision.HIGHEST
smoothing_sq = 0.25
inverse_four_pi = 0.25 / math.pi
leaf_group = 64
near_group = 32

def features(coords, frequencies, phases):
    angles = jnp.einsum('ik,ibp->bkp', frequencies, coords, precision=highest) + phases[None, :, None]
    return jnp.cos(angles)

def moments_of(coords, charged, frequencies, phases, charge_dirs):
    basis = features(coords, frequencies, phases)
    weights = jnp.einsum('ik,ibp->bkp', charge_dirs, charged, precision=highest)
    return lax.optimization_barrier(jnp.sum(basis * weights, axis=2))

def velocity_of(coords, expansion, frequencies, phases, velocity_dirs):
    basis = features(coords, frequencies, phases)
    scaled = expansion[:, :, None] * basis
    return jnp.einsum('ik,bkp->ibp', velocity_dirs, scaled, precision=highest)

def upward(maps, child):
    grouped_child = child.reshape(-1, 8, child.shape[-1])
    return jnp.einsum('jkl,qjl->qk', maps, grouped_child, precision=highest)

def downward(maps, parent):
    return jnp.einsum('jkl,ql->qjk', maps, parent, precision=highest).reshape(-1, parent.shape[-1])

def translate(maps, classes, sources):
    onehot = (classes[:, :, None] == jnp.arange(maps.shape[0], dtype=jnp.int32)[None, None, :]).astype(jnp.float32)
    summed = jnp.einsum('bln,blk->nbk', onehot, sources, precision=highest)
    return jnp.einsum('nkl,nbl->bk', maps, summed, precision=highest)

def coarse_translate(maps, classes, sources):
    onehot = (classes[:, :, None] == jnp.arange(maps.shape[0], dtype=jnp.int32)[None, None, :]).astype(jnp.float32)
    summed = jnp.einsum('ten,ek->ntk', onehot, sources, precision=highest)
    return jnp.einsum('nkl,ntl->tk', maps, summed, precision=highest)

def cross_sum(targets, sources, source_strength):
    diff = targets[:, :, :, None] - sources[:, :, None, :]
    dist = lax.optimization_barrier(jnp.sum(diff * diff, axis=0)) + smoothing_sq
    kernel = inverse_four_pi / (dist * jnp.sqrt(dist))
    alpha = source_strength[:, :, None, :]
    first = alpha[1] * diff[2] - alpha[2] * diff[1]
    second = alpha[2] * diff[0] - alpha[0] * diff[2]
    third = alpha[0] * diff[1] - alpha[1] * diff[0]
    return jnp.stack([lax.optimization_barrier(jnp.sum(first * kernel, axis=-1)), lax.optimization_barrier(jnp.sum(second * kernel, axis=-1)), lax.optimization_barrier(jnp.sum(third * kernel, axis=-1))])

def near_field(ext_coords, ext_charged, near_rows, margin):
    box_total = near_rows.shape[0]
    own_rows = margin + jnp.arange(box_total, dtype=jnp.int32)
    listed = jnp.concatenate([own_rows[:, None], near_rows.astype(jnp.int32)], axis=1)

    def block(start_box):
        chosen = lax.dynamic_slice_in_dim(listed, start_box, near_group, 0)
        targets = lax.dynamic_slice_in_dim(ext_coords, start_box + margin, near_group, 1)
        total = jnp.zeros(targets.shape, jnp.float32)
        for column in range(listed.shape[1]):
            rows_here = chosen[:, column]
            src_coords = jnp.take(ext_coords, rows_here, axis=1)
            src_charged = jnp.take(ext_charged, rows_here, axis=1)
            total = total + cross_sum(targets, src_coords, src_charged)
        return total
    starts = jnp.arange(0, box_total, near_group, dtype=jnp.int32)
    pieces = lax.map(block, starts)
    return jnp.transpose(pieces, (1, 0, 2, 3)).reshape(3, box_total, -1)

def leaf_blocks(coords):
    return jnp.transpose(coords.reshape(3, -1, leaf_group, coords.shape[-1]), (1, 0, 2, 3))

def reference(positions, strengths, counts, frequencies, phases, charge_dirs, velocity_dirs, up_maps, down_maps, far_maps, coarse_maps, send_boxes, far_source, far_class, near_source, coarse_class):
    slot_index = jnp.arange(P_SIZE, dtype=jnp.int32)
    occupied = (slot_index[None, :] < counts[:, None]).astype(jnp.float32)
    charged = strengths * occupied[None]
    blocks_pos = leaf_blocks(positions)
    blocks_charge = leaf_blocks(charged)
    leaf_moments = lax.map(lambda blocks_in: moments_of(blocks_in[0], blocks_in[1], frequencies, phases, charge_dirs), (blocks_pos, blocks_charge)).reshape(BOXES, K)
    top_moments = upward(up_maps, upward(up_maps, leaf_moments))
    coarse_locals = coarse_translate(coarse_maps, coarse_class, top_moments)
    leaf_down = downward(down_maps, downward(down_maps, coarse_locals))
    device_moments = leaf_moments.reshape(NODES, B_DEV, K)
    padded_moments = jnp.pad(leaf_moments, ((MH, MH), (0, 0)))
    routed = send_boxes.reshape(NODES, NODES, CAP)
    device_ids = jnp.arange(NODES, dtype=jnp.int32)

    def far_device(inputs):
        device, source_rows, class_rows = inputs
        picked = routed[:, device, :]
        arrived = device_moments[device_ids[:, None], picked].reshape(NODES * CAP, K)
        start = (device * B_DEV).astype(jnp.int32)
        nearby = lax.dynamic_slice_in_dim(padded_moments, start, B_DEV + 2 * MH, 0)
        lookup = jnp.concatenate([nearby, arrived], axis=0)
        return translate(far_maps, class_rows, lookup[source_rows])
    leaf_far = lax.map(far_device, (device_ids, far_source.reshape(NODES, B_DEV, NL), far_class.reshape(NODES, B_DEV, NL))).reshape(BOXES, K)
    leaf_locals = leaf_down + leaf_far
    far_velocity = lax.map(lambda blocks_in: velocity_of(blocks_in[0], blocks_in[1], frequencies, phases, velocity_dirs), (blocks_pos, leaf_locals.reshape(-1, leaf_group, K)))
    far_velocity = jnp.transpose(far_velocity, (1, 0, 2, 3)).reshape(3, BOXES, P_SIZE)
    padded_pos = jnp.pad(positions, ((0, 0), (HW, HW), (0, 0)))
    padded_charge = jnp.pad(charged, ((0, 0), (HW, HW), (0, 0)))

    def near_device(inputs):
        device, near_rows = inputs
        start = (device * B_DEV).astype(jnp.int32)
        ext_pos = lax.dynamic_slice_in_dim(padded_pos, start, B_DEV + 2 * HW, 1)
        ext_charge = lax.dynamic_slice_in_dim(padded_charge, start, B_DEV + 2 * HW, 1)
        return near_field(ext_pos, ext_charge, near_rows, HW)
    near_velocity = lax.map(near_device, (device_ids, near_source.reshape(NODES, B_DEV, NN)))
    near_velocity = jnp.transpose(near_velocity, (1, 0, 2, 3)).reshape(3, BOXES, P_SIZE)
    return (far_velocity + near_velocity) * occupied[None]
```

```python
import functools
import math

import jax
import jax.numpy as jnp
import numpy as np
from jax import lax
from jax.experimental import pallas as pl
from jax.experimental.pallas import tpu as pltpu
from jax.sharding import PartitionSpec as P

HW = 4
highest = lax.Precision.HIGHEST
smoothing_sq = 0.25
inverse_four_pi = 0.25 / math.pi
GROUP = 16
ROWS = 8
f32 = jnp.float32
bf16 = jnp.bfloat16


def cosine_coefficients(degree):
    nodes = np.cos(np.pi * (np.arange(4000) + 0.5) / 4000)
    square = (nodes + 1) / 8
    fit = np.polynomial.chebyshev.Chebyshev.fit(
        square, np.cos(2 * np.pi * np.sqrt(square)), degree, domain=[0, 0.25]
    )
    return [float(c) for c in fit.convert(kind=np.polynomial.Polynomial).coef]


cos_coef = cosine_coefficients(5)


def cos_turns(turns):
    rest = turns - jnp.round(turns)
    square = rest * rest
    value = jnp.full_like(square, cos_coef[-1])
    for c in cos_coef[-2::-1]:
        value = value * square + c
    return value


def split3(x):
    h = x.astype(bf16).astype(f32)
    rest = x - h
    m = rest.astype(bf16).astype(f32)
    return h, m, rest - m


def split3_outside(x):
    h = lax.reduce_precision(x, 8, 7)
    m = lax.reduce_precision(x - h, 8, 7)
    return h, m, lax.reduce_precision(x - h - m, 8, 7)


def nt(a, b):
    return lax.dot_general(a, b, (((1,), (1,)), ((), ())), preferred_element_type=f32)


def tn(a, b):
    return lax.dot_general(a, b, (((0,), (0,)), ((), ())), preferred_element_type=f32)


def pieces(out):
    return out[0:8] + out[8:16] + out[16:24]


def moments_kernel(pq_ref, freq_ref, dirs_ref, moment_ref, basis_ref):
    def pair(j, _):
        stacks, lhs = [], []
        for o in range(2):
            h, m, l = split3(pq_ref[2 * j + o])
            stacks.append(jnp.concatenate([h, m, l, h, m, h], axis=0).astype(bf16))
            lhs.append(jnp.concatenate([h, m, l, jnp.zeros_like(h)], axis=0).astype(bf16))
        turns = jnp.dot(
            freq_ref[...], jnp.concatenate(stacks, axis=1), preferred_element_type=f32
        )
        basis = cos_turns(turns)
        high = basis.astype(bf16)
        low = (basis - high.astype(f32)).astype(bf16)
        for o in range(2):
            both = jnp.concatenate(
                [high[:, o * 128 : (o + 1) * 128], low[:, o * 128 : (o + 1) * 128]], axis=0
            )
            basis_ref[2 * j + o] = both
            got = pieces(nt(lhs[o], both))
            got = got[:, :128] + got[:, 128:]
            moment_ref[pl.ds(2 * j + o, 1), :] = jnp.sum(
                got * dirs_ref[...], axis=0, keepdims=True
            )
        return 0

    lax.fori_loop(0, GROUP // 2, pair, 0, unroll=4)


def leaf_moments_of(pq, freq, dirs):
    boxes = pq.shape[0]
    return pl.pallas_call(
        moments_kernel,
        grid=(boxes // GROUP,),
        in_specs=[
            pl.BlockSpec((GROUP, ROWS, 128), lambda i: (i, 0, 0)),
            pl.BlockSpec(freq.shape, lambda i: (0, 0)),
            pl.BlockSpec(dirs.shape, lambda i: (0, 0)),
        ],
        out_specs=[
            pl.BlockSpec((GROUP, 128), lambda i: (i, 0)),
            pl.BlockSpec((GROUP, 256, 128), lambda i: (i, 0, 0)),
        ],
        out_shape=[
            jax.ShapeDtypeStruct((boxes, 128), f32),
            jax.ShapeDtypeStruct((boxes, 256, 128), bf16),
        ],
        compiler_params=pltpu.CompilerParams(vmem_limit_bytes=32 << 20),
        cost_estimate=pl.CostEstimate(
            flops=boxes * 128 * 128 * 96, bytes_accessed=boxes * 72000, transcendentals=0
        ),
        name="leaf_moments",
    )(pq, freq, dirs)


def near_kernel(near_ref, ext_ref, out_ref, source_ref, target_ref, charge_ref):
    row = lax.broadcasted_iota(jnp.int32, (8, 128), 0)

    def prepare(s, _):
        v = ext_ref[s]
        x, y, z = v[0:1], v[1:2], v[2:3]
        a0, a1, a2 = v[3:4], v[4:5], v[5:6]
        norm = x * x + y * y + z * z
        src = jnp.where(row < 3, v, jnp.where(row == 3, norm, jnp.where(row == 4, 1.0, 0.0)))
        tgt = jnp.where(
            row < 3,
            -2.0 * v,
            jnp.where(row == 3, 1.0, jnp.where(row == 4, norm + smoothing_sq, 0.0)),
        )
        zero = jnp.zeros_like(x)
        chg = jnp.concatenate(
            [a0, a1, a2, a1 * z - a2 * y, a2 * x - a0 * z, a0 * y - a1 * x, zero, zero], axis=0
        )
        h, m, l = split3(src)
        source_ref[s] = jnp.concatenate([h, m, l, h, m, h], axis=0).astype(bf16)
        h, m, l = split3(tgt)
        target_ref[s] = jnp.concatenate([h, h, h, m, m, l], axis=0).astype(bf16)
        h, m, l = split3(chg)
        charge_ref[s] = jnp.concatenate([h, m, l, jnp.zeros_like(h)], axis=0).astype(bf16)
        return 0

    lax.fori_loop(0, ext_ref.shape[0], prepare, 0, unroll=4)

    def box(b, _):
        rows = [b + HW, near_ref[2 * b], near_ref[2 * b + 1]]
        src = jnp.concatenate([source_ref[r] for r in rows], axis=1)
        dist = tn(target_ref[b + HW], src)
        inv = lax.rsqrt(dist)
        kern = inv * inv * inv
        high = kern.astype(bf16)
        low = (kern - high.astype(f32)).astype(bf16)
        chg = [charge_ref[r] for r in rows]
        out_ref[b] = pieces(
            nt(jnp.concatenate(chg + chg, axis=1), jnp.concatenate([high, low], axis=1))
        )
        return 0

    lax.fori_loop(0, out_ref.shape[0], box, 0, unroll=4)


def near_sums(near_rows, ext):
    boxes = near_rows.shape[0] // 2
    total = ext.shape[0]
    return pl.pallas_call(
        near_kernel,
        grid_spec=pltpu.PrefetchScalarGridSpec(
            num_scalar_prefetch=1,
            grid=(1,),
            in_specs=[pl.BlockSpec(ext.shape, lambda i, n: (0, 0, 0))],
            out_specs=pl.BlockSpec((boxes, 8, 128), lambda i, n: (0, 0, 0)),
            scratch_shapes=[
                pltpu.VMEM((total, 48, 128), bf16),
                pltpu.VMEM((total, 48, 128), bf16),
                pltpu.VMEM((total, 32, 128), bf16),
            ],
        ),
        out_shape=jax.ShapeDtypeStruct((boxes, 8, 128), f32),
        compiler_params=pltpu.CompilerParams(vmem_limit_bytes=48 << 20),
        cost_estimate=pl.CostEstimate(
            flops=boxes * 3 * 128 * 128 * 160, bytes_accessed=boxes * 8192, transcendentals=0
        ),
        name="near_sums",
    )(near_rows, ext)


def far_kernel(
    index_ref, table_ref, maps_ref, down_ref, dirs_ref, basis_ref, near_ref, pq_ref, out_ref, moved_ref
):
    size = table_ref.shape[0]
    step = pl.program_id(0)

    @pl.when(step == 0)
    def _():
        def one(n, _):
            moved_ref[pl.ds(n * size, size), :] = lax.dot_general(
                table_ref[...],
                maps_ref[n],
                (((1,), (1,)), ((), ())),
                preferred_element_type=f32,
                precision=highest,
            )
            return 0

        lax.fori_loop(0, maps_ref.shape[0], one, 0)

    links = index_ref.shape[0] // (pl.num_programs(0) * GROUP)

    def box(j, _):
        start = (step * GROUP + j) * links
        sums = [down_ref[pl.ds(j, 1), :], None, None, None]
        for l in range(links):
            got = moved_ref[pl.ds(index_ref[start + l], 1), :]
            sums[l % 4] = got if sums[l % 4] is None else sums[l % 4] + got
        local = (sums[0] + sums[1]) + (sums[2] + sums[3])
        h, m, l = split3(dirs_ref[...] * local)
        lhs = jnp.concatenate([h, m, l, jnp.zeros_like(h)], axis=0).astype(bf16)
        far = pieces(
            jnp.dot(
                jnp.concatenate([lhs, lhs], axis=1), basis_ref[j], preferred_element_type=f32
            )
        )
        pq = pq_ref[j]
        near = near_ref[j]
        x, y, z, keep = pq[0:1], pq[1:2], pq[2:3], pq[6:7]
        s0, s1, s2 = near[0:1], near[1:2], near[2:3]
        first = s1 * z - s2 * y - near[3:4]
        second = s2 * x - s0 * z - near[4:5]
        third = s0 * y - s1 * x - near[5:6]
        for i, value in enumerate((first, second, third)):
            out_ref[i, pl.ds(j, 1), :] = (far[i : i + 1] + value * inverse_four_pi) * keep
        return 0

    lax.fori_loop(0, GROUP, box, 0, unroll=4)


def far_velocity_of(index, table, maps, down, dirs, basis, near, pq):
    boxes = pq.shape[0]
    return pl.pallas_call(
        far_kernel,
        grid_spec=pltpu.PrefetchScalarGridSpec(
            num_scalar_prefetch=1,
            grid=(boxes // GROUP,),
            in_specs=[
                pl.BlockSpec(table.shape, lambda i, n: (0, 0)),
                pl.BlockSpec(maps.shape, lambda i, n: (0, 0, 0)),
                pl.BlockSpec((GROUP, 128), lambda i, n: (i, 0)),
                pl.BlockSpec(dirs.shape, lambda i, n: (0, 0)),
                pl.BlockSpec((GROUP, 256, 128), lambda i, n: (i, 0, 0)),
                pl.BlockSpec((GROUP, 8, 128), lambda i, n: (i, 0, 0)),
                pl.BlockSpec((GROUP, 8, 128), lambda i, n: (i, 0, 0)),
            ],
            out_specs=pl.BlockSpec((3, GROUP, 128), lambda i, n: (0, i, 0)),
            scratch_shapes=[pltpu.VMEM((maps.shape[0] * table.shape[0], 128), f32)],
        ),
        out_shape=jax.ShapeDtypeStruct((3, boxes, 128), f32),
        compiler_params=pltpu.CompilerParams(vmem_limit_bytes=48 << 20),
        name="far_velocity",
    )(index, table, maps, down, dirs, basis, near, pq)


def padded(cells, axis, width):
    count = lax.axis_size(axis)
    ends = count - 1
    head = cells[:width]
    tail = cells[cells.shape[0] - width :]
    return jnp.concatenate(
        [
            lax.ppermute(tail, axis, [(i, i + 1) for i in range(ends)]),
            cells,
            lax.ppermute(head, axis, [(i + 1, i) for i in range(ends)]),
        ],
        axis=0,
    )


def upward(maps, child):
    grouped_child = child.reshape(-1, 8, child.shape[-1])
    return jnp.einsum("jkl,qjl->qk", maps, grouped_child, precision=highest)


def downward(maps, parent):
    return jnp.einsum("jkl,ql->qjk", maps, parent, precision=highest).reshape(-1, parent.shape[-1])


def coarse_translate(maps, classes, sources):
    onehot = (
        classes[:, :, None] == jnp.arange(maps.shape[0], dtype=jnp.int32)[None, None, :]
    ).astype(f32)
    summed = jnp.einsum("ten,ek->ntk", onehot, sources, precision=highest)
    return jnp.einsum("nkl,ntl->tk", maps, summed, precision=highest)


def shards(
    positions,
    strengths,
    counts,
    frequencies,
    phases,
    charge_dirs,
    velocity_dirs,
    up_maps,
    down_maps,
    far_maps,
    coarse_maps,
    send_boxes,
    far_source,
    far_class,
    near_source,
    coarse_class,
):
    axis = ("curve", "sub")
    boxes, slots = positions.shape[1:]
    coeffs = frequencies.shape[1]
    slot_index = jnp.arange(slots, dtype=jnp.int32)
    occupied = (slot_index[None, :] < counts[:, None]).astype(f32)
    charged = strengths * occupied[None]
    pq = jnp.stack(
        [positions[0], positions[1], positions[2], charged[0], charged[1], charged[2], occupied,
         jnp.ones_like(occupied)],
        axis=1,
    )
    ext = padded(pq, axis, HW)
    none = jnp.zeros((coeffs,), f32)
    turn = 1.0 / (2.0 * math.pi)
    waves = jnp.stack(
        [frequencies[0] * turn, frequencies[1] * turn, frequencies[2] * turn, none, none, none, none,
         phases * turn],
        axis=1,
    )
    h, m, l = split3_outside(waves)
    freq = jnp.concatenate([h, h, h, m, m, l], axis=1).astype(bf16)
    dirs = jnp.stack([none, none, none, charge_dirs[0], charge_dirs[1], charge_dirs[2], none, none])
    leaf_moments, basis = leaf_moments_of(pq, freq, dirs)
    nearby_moments = padded(leaf_moments, axis, boxes // 2)
    parcel = leaf_moments[send_boxes]
    received = lax.all_to_all(parcel, axis, split_axis=0, concat_axis=0, tiled=True)
    top_moments = upward(up_maps, upward(up_maps, leaf_moments))
    coarse_moments = lax.all_gather(top_moments, axis, axis=0, tiled=True)
    near = near_sums(near_source.reshape(-1), ext)
    coarse_locals = coarse_translate(coarse_maps, coarse_class, coarse_moments)
    leaf_down = downward(down_maps, downward(down_maps, coarse_locals))
    table = jnp.concatenate([nearby_moments, received.reshape(-1, coeffs)], axis=0)
    index = (far_class * table.shape[0] + far_source).reshape(-1)
    vel_dirs = jnp.concatenate([velocity_dirs, jnp.zeros((5, coeffs), f32)], axis=0)
    return far_velocity_of(index, table, far_maps, leaf_down, vel_dirs, basis, near, pq)


def solution(mesh):
    boxed = P(None, ("runs", "curve", "sub"), None)
    listed = P(("runs", "curve", "sub"), None)
    return jax.shard_map(
        shards,
        mesh=mesh,
        in_specs=(boxed, boxed, P(("runs", "curve", "sub")), *([P()] * 8), *([listed] * 5)),
        out_specs=boxed,
        check_vma=False,
    )
```

```python
import functools
import math

import jax
import jax.numpy as jnp
import numpy as np
from jax import lax
from jax.experimental import pallas as pl
from jax.experimental.pallas import tpu as pltpu
from jax.sharding import PartitionSpec as P

HW = 4
highest = lax.Precision.HIGHEST
smoothing_sq = 0.25
inverse_four_pi = 0.25 / math.pi
ROWS = 8
f32 = jnp.float32
bf16 = jnp.bfloat16


def cosine_coefficients(degree):
    nodes = np.cos(np.pi * (np.arange(4000) + 0.5) / 4000)
    square = (nodes + 1) / 8
    fit = np.polynomial.chebyshev.Chebyshev.fit(
        square, np.cos(2 * np.pi * np.sqrt(square)), degree, domain=[0, 0.25]
    )
    return [float(c) for c in fit.convert(kind=np.polynomial.Polynomial).coef]


cos_coef = cosine_coefficients(5)


def cos_turns(turns):
    rest = turns - jnp.round(turns)
    square = rest * rest
    value = jnp.full_like(square, cos_coef[-1])
    for c in cos_coef[-2::-1]:
        value = value * square + c
    return value


def split3(x):
    h = x.astype(bf16).astype(f32)
    rest = x - h
    m = rest.astype(bf16).astype(f32)
    return h, m, rest - m


def split3_outside(x):
    h = lax.reduce_precision(x, 8, 7)
    m = lax.reduce_precision(x - h, 8, 7)
    return h, m, lax.reduce_precision(x - h - m, 8, 7)


def nt(a, b):
    return lax.dot_general(a, b, (((1,), (1,)), ((), ())), preferred_element_type=f32)


def tn(a, b):
    return lax.dot_general(a, b, (((0,), (0,)), ((), ())), preferred_element_type=f32)


def pieces(out):
    return out[0:8] + out[8:16] + out[16:24]


def stacks_of(tile):
    h, m, l = split3(tile)
    angles = jnp.concatenate([h, m, l, h, m, h], axis=0).astype(bf16)
    return angles, jnp.concatenate([h, m, l, jnp.zeros_like(h)], axis=0).astype(bf16)


def split_product(lhs, rhs):
    high = rhs.astype(bf16)
    low = (rhs - high.astype(f32)).astype(bf16)
    out = jnp.dot(
        jnp.concatenate([lhs, lhs], axis=1),
        jnp.concatenate([high, low], axis=0),
        preferred_element_type=f32,
    )
    return pieces(out)


def moments_kernel(pq_ref, freq_ref, dirs_ref, moment_ref):
    def box(b, _):
        angles, charges = stacks_of(pq_ref[b])
        got = split_product(charges, cos_turns(tn(angles, freq_ref[...])))
        moment_ref[pl.ds(b, 1), :] = jnp.sum(got * dirs_ref[...], axis=0, keepdims=True)
        return 0

    lax.fori_loop(0, pq_ref.shape[0], box, 0, unroll=32)


def leaf_moments_of(pq, freq, dirs):
    boxes = pq.shape[0]
    return pl.pallas_call(
        moments_kernel,
        out_shape=jax.ShapeDtypeStruct((boxes, 128), f32),
        compiler_params=pltpu.CompilerParams(vmem_limit_bytes=32 << 20),
        cost_estimate=pl.CostEstimate(
            flops=boxes * 128 * 128 * 96, bytes_accessed=boxes * 8192, transcendentals=0
        ),
        name="leaf_moments",
    )(pq, freq, dirs)


def near_kernel(near_ref, ext_ref, out_ref, source_ref, target_ref, charge_ref):
    row = lax.broadcasted_iota(jnp.int32, (8, 128), 0)

    def prepare(s, _):
        v = ext_ref[s]
        x, y, z = v[0:1], v[1:2], v[2:3]
        a0, a1, a2 = v[3:4], v[4:5], v[5:6]
        norm = x * x + y * y + z * z
        src = jnp.where(row < 3, v, jnp.where(row == 3, norm, jnp.where(row == 4, 1.0, 0.0)))
        tgt = jnp.where(
            row < 3,
            -2.0 * v,
            jnp.where(row == 3, 1.0, jnp.where(row == 4, norm + smoothing_sq, 0.0)),
        )
        zero = jnp.zeros_like(x)
        chg = jnp.concatenate(
            [a0, a1, a2, a1 * z - a2 * y, a2 * x - a0 * z, a0 * y - a1 * x, zero, zero], axis=0
        )
        h, m, l = split3(src)
        source_ref[s] = jnp.concatenate([h, m, l, h, m, h], axis=0).astype(bf16)
        h, m, l = split3(tgt)
        target_ref[s] = jnp.concatenate([h, h, h, m, m, l], axis=0).astype(bf16)
        h, m, l = split3(chg)
        charge_ref[s] = jnp.concatenate([h, m, l, jnp.zeros_like(h)], axis=0).astype(bf16)
        return 0

    lax.fori_loop(0, ext_ref.shape[0], prepare, 0, unroll=4)

    def box(b, _):
        rows = [b + HW, near_ref[2 * b], near_ref[2 * b + 1]]
        src = jnp.concatenate([source_ref[r] for r in rows], axis=1)
        inv = lax.rsqrt(tn(src, target_ref[b + HW]))
        charges = jnp.concatenate([charge_ref[r] for r in rows], axis=1)
        out_ref[b] = split_product(charges, inv * inv * inv)
        return 0

    lax.fori_loop(0, out_ref.shape[0], box, 0, unroll=32)


def near_sums(near_rows, ext):
    boxes = near_rows.shape[0] // 2
    total = ext.shape[0]
    return pl.pallas_call(
        near_kernel,
        grid_spec=pltpu.PrefetchScalarGridSpec(
            num_scalar_prefetch=1,
            grid=(1,),
            in_specs=[pl.BlockSpec(ext.shape, lambda i, n: (0, 0, 0))],
            out_specs=pl.BlockSpec((boxes, 8, 128), lambda i, n: (0, 0, 0)),
            scratch_shapes=[
                pltpu.VMEM((total, 48, 128), bf16),
                pltpu.VMEM((total, 48, 128), bf16),
                pltpu.VMEM((total, 32, 128), bf16),
            ],
        ),
        out_shape=jax.ShapeDtypeStruct((boxes, 8, 128), f32),
        compiler_params=pltpu.CompilerParams(vmem_limit_bytes=48 << 20),
        cost_estimate=pl.CostEstimate(
            flops=boxes * 3 * 128 * 128 * 160, bytes_accessed=boxes * 8192, transcendentals=0
        ),
        name="near_sums",
    )(near_rows, ext)


def far_kernel(
    index_ref, table_ref, maps_ref, down_ref, freq_ref, dirs_ref, near_ref, pq_ref, out_ref, moved_ref
):
    size = table_ref.shape[0]
    high = table_ref[...].astype(bf16)
    both = jnp.concatenate([high, (table_ref[...] - high.astype(f32)).astype(bf16)], axis=1)

    def one(n, _):
        got = jnp.dot(both, maps_ref[n], preferred_element_type=f32)
        moved_ref[pl.ds(pl.multiple_of(n * size, size), size), :] = got[:, :128] + got[:, 128:]
        return 0

    lax.fori_loop(0, maps_ref.shape[0], one, 0)
    boxes = pq_ref.shape[0]
    links = index_ref.shape[0] // boxes

    def box(b, _):
        sums = [down_ref[pl.ds(b, 1), :], None, None, None]
        for l in range(links):
            got = moved_ref[pl.ds(index_ref[b * links + l], 1), :]
            sums[l % 4] = got if sums[l % 4] is None else sums[l % 4] + got
        local = (sums[0] + sums[1]) + (sums[2] + sums[3])
        pq = pq_ref[b]
        angles, _ = stacks_of(pq)
        _, weights = stacks_of(dirs_ref[...] * local)
        turns = jnp.dot(freq_ref[...], angles, preferred_element_type=f32)
        far = split_product(weights, cos_turns(turns))
        near = near_ref[b]
        x, y, z, keep = pq[0:1], pq[1:2], pq[2:3], pq[6:7]
        s0, s1, s2 = near[0:1], near[1:2], near[2:3]
        first = s1 * z - s2 * y - near[3:4]
        second = s2 * x - s0 * z - near[4:5]
        third = s0 * y - s1 * x - near[5:6]
        for i, value in enumerate((first, second, third)):
            out_ref[i, pl.ds(b, 1), :] = (far[i : i + 1] + value * inverse_four_pi) * keep
        return 0

    lax.fori_loop(0, boxes, box, 0, unroll=16)


def far_velocity_of(index, table, maps, down, freq, dirs, near, pq):
    boxes = pq.shape[0]
    whole = [
        pl.BlockSpec(a.shape, functools.partial(lambda rank, i, n: (0,) * rank, a.ndim))
        for a in (table, maps, down, freq, dirs, near, pq)
    ]
    return pl.pallas_call(
        far_kernel,
        grid_spec=pltpu.PrefetchScalarGridSpec(
            num_scalar_prefetch=1,
            grid=(1,),
            in_specs=whole,
            out_specs=pl.BlockSpec((3, boxes, 128), lambda i, n: (0, 0, 0)),
            scratch_shapes=[pltpu.VMEM((maps.shape[0] * table.shape[0], 128), f32)],
        ),
        out_shape=jax.ShapeDtypeStruct((3, boxes, 128), f32),
        compiler_params=pltpu.CompilerParams(vmem_limit_bytes=48 << 20),
        name="far_velocity",
    )(index, table, maps, down, freq, dirs, near, pq)


def padded(cells, axis, width):
    count = lax.axis_size(axis)
    ends = count - 1
    head = cells[:width]
    tail = cells[cells.shape[0] - width :]
    return jnp.concatenate(
        [
            lax.ppermute(tail, axis, [(i, i + 1) for i in range(ends)]),
            cells,
            lax.ppermute(head, axis, [(i + 1, i) for i in range(ends)]),
        ],
        axis=0,
    )


def upward(maps, child):
    grouped_child = child.reshape(-1, 8, child.shape[-1])
    return jnp.einsum("jkl,qjl->qk", maps, grouped_child, precision=highest)


def downward(maps, parent):
    return jnp.einsum("jkl,ql->qjk", maps, parent, precision=highest).reshape(-1, parent.shape[-1])


def coarse_translate(maps, classes, sources):
    onehot = (
        classes[:, :, None] == jnp.arange(maps.shape[0], dtype=jnp.int32)[None, None, :]
    ).astype(f32)
    summed = jnp.einsum("ten,ek->ntk", onehot, sources, precision=highest)
    return jnp.einsum("nkl,ntl->tk", maps, summed, precision=highest)


def shards(
    positions,
    strengths,
    counts,
    frequencies,
    phases,
    charge_dirs,
    velocity_dirs,
    up_maps,
    down_maps,
    far_maps,
    coarse_maps,
    send_boxes,
    far_source,
    far_class,
    near_source,
    coarse_class,
):
    axis = ("curve", "sub")
    boxes, slots = positions.shape[1:]
    coeffs = frequencies.shape[1]
    slot_index = jnp.arange(slots, dtype=jnp.int32)
    occupied = (slot_index[None, :] < counts[:, None]).astype(f32)
    charged = strengths * occupied[None]
    pq = jnp.stack(
        [positions[0], positions[1], positions[2], charged[0], charged[1], charged[2], occupied,
         jnp.ones_like(occupied)],
        axis=1,
    )
    ext = padded(pq, axis, HW)
    none = jnp.zeros((coeffs,), f32)
    turn = 1.0 / (2.0 * math.pi)
    waves = jnp.stack(
        [frequencies[0] * turn, frequencies[1] * turn, frequencies[2] * turn, none, none, none, none,
         phases * turn],
        axis=1,
    )
    h, m, l = split3_outside(waves)
    freq = jnp.concatenate([h, h, h, m, m, l], axis=1).astype(bf16)
    dirs = jnp.stack([none, none, none, charge_dirs[0], charge_dirs[1], charge_dirs[2], none, none])
    leaf_moments = leaf_moments_of(pq, freq.T, dirs)
    nearby_moments = padded(leaf_moments, axis, boxes // 2)
    top_moments = upward(up_maps, upward(up_maps, leaf_moments))
    nodes = lax.axis_size(axis)
    listed = leaf_moments[send_boxes.reshape(nodes, -1)]
    tops = jnp.broadcast_to(top_moments[None], (nodes, *top_moments.shape))
    received = lax.all_to_all(
        jnp.concatenate([listed, tops], axis=1), axis, split_axis=0, concat_axis=0, tiled=True
    )
    reach = listed.shape[1]
    near = near_sums(near_source.reshape(-1), ext)
    coarse_moments = received[:, reach:].reshape(-1, coeffs)
    coarse_locals = coarse_translate(coarse_maps, coarse_class, coarse_moments)
    leaf_down = downward(down_maps, downward(down_maps, coarse_locals))
    table = jnp.concatenate([nearby_moments, received[:, :reach].reshape(-1, coeffs)], axis=0)
    index = (far_class * table.shape[0] + far_source).reshape(-1)
    maps_t = jnp.swapaxes(far_maps, 1, 2)
    high = lax.reduce_precision(maps_t, 8, 7)
    low = lax.reduce_precision(maps_t - high, 8, 7)
    maps = jnp.concatenate(
        [
            jnp.concatenate([high, low], axis=2),
            jnp.concatenate([high, jnp.zeros_like(low)], axis=2),
        ],
        axis=1,
    ).astype(bf16)
    vel_dirs = jnp.concatenate([velocity_dirs, jnp.zeros((5, coeffs), f32)], axis=0)
    return far_velocity_of(index, table, maps, leaf_down, freq, vel_dirs, near, pq)


def solution(mesh):
    boxed = P(None, ("runs", "curve", "sub"), None)
    listed = P(("runs", "curve", "sub"), None)
    return jax.shard_map(
        shards,
        mesh=mesh,
        in_specs=(boxed, boxed, P(("runs", "curve", "sub")), *([P()] * 8), *([listed] * 5)),
        out_specs=boxed,
        check_vma=False,
    )
```

```python
import functools
import math

import jax
import jax.numpy as jnp
import numpy as np
from jax import lax
from jax.experimental import pallas as pl
from jax.experimental.pallas import tpu as pltpu
from jax.sharding import PartitionSpec as P

HW = 4
highest = lax.Precision.HIGHEST
smoothing_sq = 0.25
inverse_four_pi = 0.25 / math.pi
ROWS = 8
f32 = jnp.float32
bf16 = jnp.bfloat16


def cosine_coefficients(degree):
    nodes = np.cos(np.pi * (np.arange(4000) + 0.5) / 4000)
    square = (nodes + 1) / 8
    fit = np.polynomial.chebyshev.Chebyshev.fit(
        square, np.cos(2 * np.pi * np.sqrt(square)), degree, domain=[0, 0.25]
    )
    return [float(c) for c in fit.convert(kind=np.polynomial.Polynomial).coef]


cos_coef = cosine_coefficients(5)


def cos_turns(turns):
    rest = turns - jnp.round(turns)
    square = rest * rest
    value = jnp.full_like(square, cos_coef[-1])
    for c in cos_coef[-2::-1]:
        value = value * square + c
    return value


def split3(x):
    h = x.astype(bf16).astype(f32)
    rest = x - h
    m = rest.astype(bf16).astype(f32)
    return h, m, rest - m


def split3_outside(x):
    h = lax.reduce_precision(x, 8, 7)
    m = lax.reduce_precision(x - h, 8, 7)
    return h, m, lax.reduce_precision(x - h - m, 8, 7)


def tn(a, b):
    return lax.dot_general(a, b, (((0,), (0,)), ((), ())), preferred_element_type=f32)


def pieces(out):
    return out[0:8] + out[8:16] + out[16:24]


def stacks_of(tile):
    h, m, l = split3(tile)
    angles = jnp.concatenate([h, m, l, h, m, h], axis=0).astype(bf16)
    return angles, jnp.concatenate([h, m, l, jnp.zeros_like(h)], axis=0).astype(bf16)


def split_product(lhs, rhs):
    high = rhs.astype(bf16)
    low = (rhs - high.astype(f32)).astype(bf16)
    out = jnp.dot(
        jnp.concatenate([lhs, lhs], axis=1),
        jnp.concatenate([high, low], axis=0),
        preferred_element_type=f32,
    )
    return pieces(out)


def moments_kernel(counts_ref, pos_ref, str_ref, freq_ref, dirs_ref, moment_ref, pq_ref):
    lane = lax.broadcasted_iota(jnp.int32, (1, 128), 1)
    one = jnp.ones((1, 128), f32)

    def box(b, _):
        keep = jnp.where(lane < counts_ref[b], 1.0, 0.0)
        coords = [pos_ref[i, pl.ds(b, 1), :] for i in range(3)]
        charged = [str_ref[i, pl.ds(b, 1), :] * keep for i in range(3)]
        tile = jnp.concatenate(coords + charged + [keep, one], axis=0)
        pq_ref[b] = tile
        angles, charges = stacks_of(tile)
        got = split_product(charges, cos_turns(tn(angles, freq_ref[...])))
        moment_ref[pl.ds(b, 1), :] = jnp.sum(got * dirs_ref[...], axis=0, keepdims=True)
        return 0

    lax.fori_loop(0, pq_ref.shape[0], box, 0, unroll=64)


def leaf_moments_of(counts, positions, strengths, freq, dirs):
    boxes = counts.shape[0]
    vmem = pl.BlockSpec(memory_space=pltpu.VMEM)
    return pl.pallas_call(
        moments_kernel,
        in_specs=[pl.BlockSpec(memory_space=pltpu.SMEM), vmem, vmem, vmem, vmem],
        out_specs=[vmem, vmem],
        out_shape=[
            jax.ShapeDtypeStruct((boxes, 128), f32),
            jax.ShapeDtypeStruct((boxes, ROWS, 128), f32),
        ],
        compiler_params=pltpu.CompilerParams(vmem_limit_bytes=32 << 20),
        cost_estimate=pl.CostEstimate(
            flops=boxes * 128 * 128 * 96, bytes_accessed=boxes * 8192, transcendentals=0
        ),
        name="leaf_moments",
    )(counts, positions, strengths, freq, dirs)


def near_kernel(near_ref, ext_ref, out_ref, source_ref, target_ref, charge_ref):
    row = lax.broadcasted_iota(jnp.int32, (8, 128), 0)

    def prepare(s, _):
        v = ext_ref[s]
        x, y, z = v[0:1], v[1:2], v[2:3]
        a0, a1, a2 = v[3:4], v[4:5], v[5:6]
        norm = x * x + y * y + z * z
        src = jnp.where(row < 3, v, jnp.where(row == 3, norm, jnp.where(row == 4, 1.0, 0.0)))
        tgt = jnp.where(
            row < 3,
            -2.0 * v,
            jnp.where(row == 3, 1.0, jnp.where(row == 4, norm + smoothing_sq, 0.0)),
        )
        zero = jnp.zeros_like(x)
        chg = jnp.concatenate(
            [a0, a1, a2, a1 * z - a2 * y, a2 * x - a0 * z, a0 * y - a1 * x, zero, zero], axis=0
        )
        h, m, l = split3(src)
        source_ref[s] = jnp.concatenate([h, m, l, h, m, h], axis=0).astype(bf16)
        h, m, l = split3(tgt)
        target_ref[s] = jnp.concatenate([h, h, h, m, m, l], axis=0).astype(bf16)
        h, m, l = split3(chg)
        charge_ref[s] = jnp.concatenate([h, m, l, jnp.zeros_like(h)], axis=0).astype(bf16)
        return 0

    lax.fori_loop(0, ext_ref.shape[0], prepare, 0, unroll=4)

    def box(b, _):
        rows = [b + HW, near_ref[2 * b], near_ref[2 * b + 1]]
        src = jnp.concatenate([source_ref[r] for r in rows], axis=1)
        inv = lax.rsqrt(tn(src, target_ref[b + HW]))
        charges = jnp.concatenate([charge_ref[r] for r in rows], axis=1)
        out_ref[b] = split_product(charges, inv * inv * inv)
        return 0

    lax.fori_loop(0, out_ref.shape[0], box, 0, unroll=64)


def near_sums(near_rows, ext):
    boxes = near_rows.shape[0] // 2
    total = ext.shape[0]
    return pl.pallas_call(
        near_kernel,
        grid_spec=pltpu.PrefetchScalarGridSpec(
            num_scalar_prefetch=1,
            grid=(1,),
            in_specs=[pl.BlockSpec(ext.shape, lambda i, n: (0, 0, 0))],
            out_specs=pl.BlockSpec((boxes, 8, 128), lambda i, n: (0, 0, 0)),
            scratch_shapes=[
                pltpu.VMEM((total, 48, 128), bf16),
                pltpu.VMEM((total, 48, 128), bf16),
                pltpu.VMEM((total, 32, 128), bf16),
            ],
        ),
        out_shape=jax.ShapeDtypeStruct((boxes, 8, 128), f32),
        compiler_params=pltpu.CompilerParams(vmem_limit_bytes=48 << 20),
        cost_estimate=pl.CostEstimate(
            flops=boxes * 3 * 128 * 128 * 160, bytes_accessed=boxes * 8192, transcendentals=0
        ),
        name="near_sums",
    )(near_rows, ext)


def far_kernel(
    index_ref, table_ref, maps_ref, down_ref, freq_ref, dirs_ref, near_ref, pq_ref, out_ref, moved_ref
):
    size = table_ref.shape[0]
    high = table_ref[...].astype(bf16)
    both = jnp.concatenate([high, (table_ref[...] - high.astype(f32)).astype(bf16)], axis=1)

    def one(n, _):
        got = jnp.dot(both, maps_ref[n], preferred_element_type=f32)
        moved_ref[pl.ds(pl.multiple_of(n * size, size), size), :] = got[:, :128] + got[:, 128:]
        return 0

    lax.fori_loop(0, maps_ref.shape[0], one, 0)
    boxes = pq_ref.shape[0]
    links = index_ref.shape[0] // boxes

    def box(b, _):
        sums = [down_ref[pl.ds(b, 1), :], None, None, None]
        for l in range(links):
            got = moved_ref[pl.ds(index_ref[b * links + l], 1), :]
            sums[l % 4] = got if sums[l % 4] is None else sums[l % 4] + got
        local = (sums[0] + sums[1]) + (sums[2] + sums[3])
        pq = pq_ref[b]
        angles, _ = stacks_of(pq)
        _, weights = stacks_of(dirs_ref[...] * local)
        turns = jnp.dot(freq_ref[...], angles, preferred_element_type=f32)
        far = split_product(weights, cos_turns(turns))
        near = near_ref[b]
        x, y, z, keep = pq[0:1], pq[1:2], pq[2:3], pq[6:7]
        s0, s1, s2 = near[0:1], near[1:2], near[2:3]
        first = s1 * z - s2 * y - near[3:4]
        second = s2 * x - s0 * z - near[4:5]
        third = s0 * y - s1 * x - near[5:6]
        for i, value in enumerate((first, second, third)):
            out_ref[i, pl.ds(b, 1), :] = (far[i : i + 1] + value * inverse_four_pi) * keep
        return 0

    lax.fori_loop(0, boxes, box, 0, unroll=32)


def far_velocity_of(index, table, maps, down, freq, dirs, near, pq):
    boxes = pq.shape[0]
    whole = [
        pl.BlockSpec(a.shape, functools.partial(lambda rank, i, n: (0,) * rank, a.ndim))
        for a in (table, maps, down, freq, dirs, near, pq)
    ]
    return pl.pallas_call(
        far_kernel,
        grid_spec=pltpu.PrefetchScalarGridSpec(
            num_scalar_prefetch=1,
            grid=(1,),
            in_specs=whole,
            out_specs=pl.BlockSpec((3, boxes, 128), lambda i, n: (0, 0, 0)),
            scratch_shapes=[pltpu.VMEM((maps.shape[0] * table.shape[0], 128), f32)],
        ),
        out_shape=jax.ShapeDtypeStruct((3, boxes, 128), f32),
        compiler_params=pltpu.CompilerParams(vmem_limit_bytes=48 << 20),
        name="far_velocity",
    )(index, table, maps, down, freq, dirs, near, pq)


def reached(moments, tiles, axis, width):
    count = lax.axis_size(axis)
    ends = count - 1
    total = moments.shape[0]
    head = jnp.concatenate([moments[:width], tiles[:HW].reshape(HW * ROWS, -1)], axis=0)
    tail = jnp.concatenate(
        [moments[total - width :], tiles[total - HW :].reshape(HW * ROWS, -1)], axis=0
    )
    before = lax.ppermute(tail, axis, [(i, i + 1) for i in range(ends)])
    after = lax.ppermute(head, axis, [(i + 1, i) for i in range(ends)])
    near_tiles = [part[width:].reshape(HW, ROWS, -1) for part in (before, after)]
    return (
        [before[:width], moments, after[:width]],
        jnp.concatenate([near_tiles[0], tiles, near_tiles[1]], axis=0),
    )


def upward(maps, child):
    grouped_child = child.reshape(-1, 8, child.shape[-1])
    return jnp.einsum("jkl,qjl->qk", maps, grouped_child, precision=highest)


def downward(maps, parent):
    return jnp.einsum("jkl,ql->qjk", maps, parent, precision=highest).reshape(-1, parent.shape[-1])


def coarse_translate(maps, classes, sources):
    onehot = (
        classes[:, :, None] == jnp.arange(maps.shape[0], dtype=jnp.int32)[None, None, :]
    ).astype(f32)
    summed = jnp.einsum("ten,ek->ntk", onehot, sources, precision=highest)
    return jnp.einsum("nkl,ntl->tk", maps, summed, precision=highest)


def shards(
    positions,
    strengths,
    counts,
    frequencies,
    phases,
    charge_dirs,
    velocity_dirs,
    up_maps,
    down_maps,
    far_maps,
    coarse_maps,
    send_boxes,
    far_source,
    far_class,
    near_source,
    coarse_class,
):
    axis = ("curve", "sub")
    boxes = positions.shape[1]
    coeffs = frequencies.shape[1]
    none = jnp.zeros((coeffs,), f32)
    turn = 1.0 / (2.0 * math.pi)
    waves = jnp.stack(
        [frequencies[0] * turn, frequencies[1] * turn, frequencies[2] * turn, none, none, none, none,
         phases * turn],
        axis=1,
    )
    h, m, l = split3_outside(waves)
    freq = jnp.concatenate([h, h, h, m, m, l], axis=1).astype(bf16)
    dirs = jnp.stack([none, none, none, charge_dirs[0], charge_dirs[1], charge_dirs[2], none, none])
    leaf_moments, pq = leaf_moments_of(counts, positions, strengths, freq.T, dirs)
    nearby_moments, ext = reached(leaf_moments, pq, axis, boxes // 2)
    top_moments = upward(up_maps, upward(up_maps, leaf_moments))
    nodes = lax.axis_size(axis)
    listed = leaf_moments[send_boxes.reshape(nodes, -1)]
    tops = jnp.broadcast_to(top_moments[None], (nodes, *top_moments.shape))
    received = lax.all_to_all(
        jnp.concatenate([listed, tops], axis=1), axis, split_axis=0, concat_axis=0, tiled=True
    )
    reach = listed.shape[1]
    near = near_sums(near_source.reshape(-1), ext)
    coarse_moments = received[:, reach:].reshape(-1, coeffs)
    coarse_locals = coarse_translate(coarse_maps, coarse_class, coarse_moments)
    leaf_down = downward(down_maps, downward(down_maps, coarse_locals))
    table = jnp.concatenate([*nearby_moments, received[:, :reach].reshape(-1, coeffs)], axis=0)
    index = (far_class * table.shape[0] + far_source).reshape(-1)
    maps_t = jnp.swapaxes(far_maps, 1, 2)
    high = lax.reduce_precision(maps_t, 8, 7)
    low = lax.reduce_precision(maps_t - high, 8, 7)
    maps = jnp.concatenate(
        [
            jnp.concatenate([high, low], axis=2),
            jnp.concatenate([high, jnp.zeros_like(low)], axis=2),
        ],
        axis=1,
    ).astype(bf16)
    vel_dirs = jnp.concatenate([velocity_dirs, jnp.zeros((5, coeffs), f32)], axis=0)
    return far_velocity_of(index, table, maps, leaf_down, freq, vel_dirs, near, pq)


def solution(mesh):
    boxed = P(None, ("runs", "curve", "sub"), None)
    listed = P(("runs", "curve", "sub"), None)
    return jax.shard_map(
        shards,
        mesh=mesh,
        in_specs=(boxed, boxed, P(("runs", "curve", "sub")), *([P()] * 8), *([listed] * 5)),
        out_specs=boxed,
        check_vma=False,
    )
```
